32 devices in a mesh: grp: 2 (over y), tok: 8 (over z, core), head: 2 (over x).
Axes of the slice: x: 2, y: 2, z: 4, core: 2. Of those that a mesh axis runs over, the one named last changes fastest.
Arguments:
- queries: bfloat16 [2, 8192, 1280], P(None, ('grp', 'tok'), 'head'), parts along dimension 1, may hold values from -6 to 6
- key_tokens: bfloat16 [2, 8192, 1280], P(None, ('grp', 'tok'), 'head'), parts along dimension 1, may hold values from -6 to 6
- values: bfloat16 [2, 8192, 1280], P(None, ('grp', 'tok'), 'head'), parts along dimension 1, may hold values from -6 to 6
- learn_rates: float32 [2, 2, 8192], P(None, 'head', ('grp', 'tok')), parts along dimension 2, may hold values from 0.03 to 0.3
- w_first: float32 [2, 640, 640], P('head'), may hold values from -0.25 to 0.25
- w_second: float32 [2, 640, 640], P('head'), may hold values from -0.25 to 0.25
- w_third: float32 [2, 640, 640], P('head'), may hold values from -0.25 to 0.25
Outputs:
- layer_output: bfloat16 [2, 8192, 1280], P(None, ('grp', 'tok', 'head')), parts along dimension 1
The draws below stay inside these ranges and needn't reach their ends.
There are 2 independent parts, one for each index of `grp`. The reference program is written for one: setup_inputs(seed, part) draws one part's arguments, and reference() takes and returns one part's arrays. A program takes and returns all parts, laid end to end along the dimension named above; an argument that names none is the same for every part. Nothing has to cross between parts.
All inputs are finite; a program needn't handle non-finite values.
Results may differ from the reference program's by a relative error of at most 0.038.
Values may be sent and summed in bfloat16 or wider, within the bound.
A program may use at most 64 MiB of HBM per device.

```python
import math
import jax
import jax.numpy as jnp
from jax import lax

HD = 640
F = 640
GROUPS = 2
HEADS = 2
GROUP_TOK = 4096


def levels(key, shape, cuts, least, largest):
    loudness = 1.0
    for dim, blocks in cuts:
        draws = jax.random.uniform(jax.random.fold_in(jax.random.fold_in(key, 6), dim), (blocks,), jnp.float32, least / len(cuts), largest / len(cuts))
        loudness = loudness * jnp.repeat(jnp.exp(draws), shape[dim] // blocks).reshape((-1,) + (1,) * (len(shape) - 1 - dim))
    return loudness


def gaussian(key, shape, width, most, split=(), held_as=jnp.bfloat16):
    entries = width * jax.random.normal(key, shape, jnp.float32)
    if split:
        entries = entries * levels(key, shape, split, -0.22, 0.18)
    return jnp.clip(entries, -most, most).astype(held_as)


def setup_inputs(seed: int = 0, part: int = 0) -> dict:
    key_list = jax.random.split(jax.random.key(seed), 8)
    own_keys = jax.random.split(jax.random.fold_in(key_list[7], part), 8)
    queries = gaussian(own_keys[0], (GROUPS, GROUP_TOK, HEADS * HD), 1.0, 6.0, ((1, 8), (2, 2)))
    key_tokens = gaussian(own_keys[1], (GROUPS, GROUP_TOK, HEADS * HD), 1.0, 6.0, ((1, 8), (2, 2)))
    values = gaussian(own_keys[2], (GROUPS, GROUP_TOK, HEADS * HD), 1.0, 6.0, ((1, 8), (2, 2)))
    learn_rates = jnp.clip(jnp.exp(math.log(0.3) - 2.3025852 * jax.random.uniform(own_keys[3], (GROUPS, HEADS, GROUP_TOK), jnp.float32) ** levels(own_keys[3], (GROUPS, HEADS, GROUP_TOK), ((1, 2), (2, 8)), -0.2, 0.2)), 0.03, 0.3)
    w_first = gaussian(key_list[4], (HEADS, F, HD), HD ** -0.5, 0.25, ((0, 2),), jnp.float32)
    w_second = gaussian(key_list[5], (HEADS, HD, F), F ** -0.5, 0.25, ((0, 2),), jnp.float32)
    w_third = gaussian(key_list[6], (HEADS, F, HD), HD ** -0.5, 0.25, ((0, 2),), jnp.float32)
    return {"queries": queries, "key_tokens": key_tokens, "values": values, "learn_rates": learn_rates, "w_first": w_first, "w_second": w_second, "w_third": w_third}


MOMENTUM_DECAY = 0.9
EPSILON = 1e-06
CONTRACT_ROWS = (((0,), (0,)), ((), ()))
CONTRACT_LAST = (((1,), (1,)), ((), ()))

def silu_slope(pre_act):
    sigmoid_value = jax.nn.sigmoid(pre_act)
    return sigmoid_value * (1.0 + pre_act * (1.0 - sigmoid_value))

def row_rms(matrix):
    return jnp.sqrt(lax.optimization_barrier(jnp.mean(matrix * matrix, axis=-1, keepdims=True)) + EPSILON)

def block_terms(keys_now, values_now, rates_now, first_b, second_b, third_b):
    pre_gate = lax.dot_general(keys_now, first_b, CONTRACT_LAST, preferred_element_type=jnp.float32)
    pre_up = lax.dot_general(keys_now, third_b, CONTRACT_LAST, preferred_element_type=jnp.float32)
    hidden = (jax.nn.silu(pre_gate) * pre_up).astype(jnp.bfloat16)
    scaled = (rates_now[:, None] * values_now.astype(jnp.float32)).astype(jnp.bfloat16)
    back_prop = jnp.dot(scaled, second_b, preferred_element_type=jnp.float32)
    grad_gate = (back_prop * pre_up * silu_slope(pre_gate)).astype(jnp.bfloat16)
    grad_up = (back_prop * jax.nn.silu(pre_gate)).astype(jnp.bfloat16)
    return (hidden, scaled, grad_gate, grad_up)

def weight_grads(gate_part, scaled_part, up_part, keys_now, hidden):
    grad_first = lax.dot_general(gate_part, keys_now, CONTRACT_ROWS, preferred_element_type=jnp.float32)
    grad_second = lax.dot_general(scaled_part, hidden, CONTRACT_ROWS, preferred_element_type=jnp.float32)
    grad_third = lax.dot_general(up_part, keys_now, CONTRACT_ROWS, preferred_element_type=jnp.float32)
    return (grad_first, grad_second, grad_third)

def apply_weights(queries_now, first_b, second_b, third_b):
    pre_gate = lax.dot_general(queries_now, first_b, CONTRACT_LAST, preferred_element_type=jnp.float32)
    pre_up = lax.dot_general(queries_now, third_b, CONTRACT_LAST, preferred_element_type=jnp.float32)
    hidden = (jax.nn.silu(pre_gate) * pre_up).astype(jnp.bfloat16)
    return lax.dot_general(hidden, second_b, CONTRACT_LAST, preferred_element_type=jnp.float32).astype(jnp.bfloat16)

def one_head(head_queries, head_keys, head_values, head_rates, first, second, third):
    current = [first, second, third]
    targets = [row_rms(matrix) for matrix in current]
    moment = [jnp.zeros_like(matrix) for matrix in current]
    grad_scale = 1.0 / math.sqrt(GROUP_TOK)
    rounded = [matrix.astype(jnp.bfloat16) for matrix in current]
    produced = []
    for block_index in range(GROUPS):
        keys_now = head_keys[block_index]
        hidden, scaled, grad_gate, grad_up = block_terms(keys_now, head_values[block_index], head_rates[block_index], rounded[0], rounded[1], rounded[2])
        grads = weight_grads(grad_gate, scaled, grad_up, keys_now, hidden)
        for index in range(3):
            moment[index] = MOMENTUM_DECAY * moment[index] + grads[index] * grad_scale
            summed = current[index] + moment[index]
            current[index] = summed * targets[index] / row_rms(summed)
        rounded = [matrix.astype(jnp.bfloat16) for matrix in current]
        produced.append(apply_weights(head_queries[block_index], rounded[0], rounded[1], rounded[2]))
    return jnp.stack(produced)

def reference(queries, key_tokens, values, learn_rates, w_first, w_second, w_third):
    head_outputs = []
    for head_index in range(HEADS):
        head_cols = slice(head_index * HD, (head_index + 1) * HD)
        head_outputs.append(one_head(queries[:, :, head_cols], key_tokens[:, :, head_cols], values[:, :, head_cols], learn_rates[:, head_index], w_first[head_index], w_second[head_index], w_third[head_index]))
    return jnp.concatenate(head_outputs, axis=2)
```

```python
import functools
import math

import jax
import jax.numpy as jnp
from jax import lax
from jax.experimental import pallas as pl
from jax.experimental.pallas import tpu as pltpu
from jax.sharding import PartitionSpec as P

MOMENTUM_DECAY = 0.9
EPSILON = 1e-06
CONTRACT_ROWS = (((0,), (0,)), ((), ()))
CONTRACT_LAST = (((1,), (1,)), ((), ()))
MESH = pl.DeviceIdType.MESH
CORES = 2
GATE, OUT, UP = 0, 1, 2
SPACING = 2


def row_rms(matrix):
    return jnp.sqrt(jnp.mean(matrix * matrix, axis=-1, keepdims=True) + EPSILON)


def dot(lhs, rhs, dims):
    return lax.dot_general(lhs, rhs, dims, preferred_element_type=jnp.float32)


def kernel(
    tok_count, head_count, share, inner,
    q_hbm, k_hbm, v_hbm, rates_ref, w1_hbm, w2_hbm, w3_hbm, out_ref,
    q_ref, k_ref, v_ref, w_ref, weights, silu_s, slope_s, e_s, z_s, ga_s, gb_s,
    grads, pair_in, from_left, from_right, cur_s, mom_s, made,
    load_sem, pair_send, pair_recv, r_send, r_recv, l_send, l_recv,
    agr_send, agl_send, ag_recv, agp_send, agp_recv, out_send, out_recv,
):
    line = tok_count // CORES
    half = line * share
    blocks, tokens, width = q_ref.shape
    slab = tokens // head_count
    tile = min(256, tokens)
    grad_scale = 1.0 / math.sqrt(tokens * tok_count)
    tok = lax.axis_index("tok")
    head = lax.axis_index("head")
    z = tok // CORES
    core = lax.rem(tok, CORES)
    mate = tok + 1 - 2 * core
    has_left = z > 0
    has_right = z < line - 1
    left, right = tok - CORES, tok + CORES

    def rows_of(owner, of_core):
        return pl.ds(pl.multiple_of((of_core * line + owner) * share, share), share)

    def in_half(owner):
        return pl.ds(pl.multiple_of(owner * share, share), share)

    barrier = pltpu.get_barrier_semaphore()

    @pl.when(has_left)
    def _():
        pl.semaphore_signal(barrier, inc=1, device_id={"tok": left}, device_id_type=MESH)

    @pl.when(has_right)
    def _():
        pl.semaphore_signal(barrier, inc=1, device_id={"tok": right}, device_id_type=MESH)

    pl.semaphore_signal(barrier, inc=1, device_id={"tok": mate}, device_id_type=MESH)
    for step in range(1, head_count):
        pl.semaphore_signal(
            barrier, inc=1, device_id={"head": lax.rem(head + step, head_count)}, device_id_type=MESH
        )

    loads = {}
    order = [
        ("k0", k_hbm.at[0], k_ref.at[0]),
        ("w1", w1_hbm, w_ref.at[GATE]),
        ("w3", w3_hbm, w_ref.at[UP]),
        ("v0", v_hbm.at[0], v_ref.at[0]),
        ("w2", w2_hbm, w_ref.at[OUT]),
    ]
    for b in range(1, blocks):
        order.append((f"k{b}", k_hbm.at[b], k_ref.at[b]))
        order.append((f"v{b}", v_hbm.at[b], v_ref.at[b]))
    for b in range(blocks):
        order.append((f"q{b}", q_hbm.at[b], q_ref.at[b]))
    for place, (name, src, dst) in enumerate(order):
        loads[name] = pltpu.make_async_copy(src, dst, load_sem.at[place])
        loads[name].start()

    def round_weights(m):
        weights[0, m] = w_ref[m].astype(jnp.bfloat16)

    def keys_part(b):
        @pl.loop(0, tokens // tile)
        def _(i):
            rows = pl.ds(pl.multiple_of(i * tile, tile), tile)
            keys = k_ref[b, rows]
            gate = dot(keys, weights[b, GATE, :inner], CONTRACT_LAST)
            up = dot(keys, weights[b, UP, :inner], CONTRACT_LAST)
            sig = jax.nn.sigmoid(gate)
            silu = gate * sig
            z_s[rows] = (silu * up).astype(jnp.bfloat16)
            silu_s[rows] = silu
            slope_s[rows] = up * (sig * (1.0 + gate * (1.0 - sig)))

    def scaled_part(b):
        lanes = math.gcd(width, 128)
        for i in range(tokens // tile):
            rows = pl.ds(i * tile, tile)
            rate = jnp.transpose(jnp.broadcast_to(rates_ref[b, :, rows], (lanes, tile)))
            for j in range(width // lanes):
                cols = pl.ds(j * lanes, lanes)
                e_s[rows, cols] = (rate * v_ref[b, rows, cols].astype(jnp.float32)).astype(jnp.bfloat16)

    def back_part(b):
        @pl.loop(0, tokens // tile)
        def _(i):
            rows = pl.ds(pl.multiple_of(i * tile, tile), tile)
            back = lax.dot_general(
                e_s[rows], weights[b, OUT, :inner], (((1,), (0,)), ((), ())),
                preferred_element_type=jnp.float32,
            )
            ga_s[rows] = (back * slope_s[rows]).astype(jnp.bfloat16)
            gb_s[rows] = (back * silu_s[rows]).astype(jnp.bfloat16)

    def grad_part(b, m):
        if m == GATE:
            value = dot(ga_s[...], k_ref[b], CONTRACT_ROWS)
        elif m == OUT:
            value = dot(e_s[...], z_s[...], CONTRACT_ROWS)
        else:
            value = dot(gb_s[...], k_ref[b], CONTRACT_ROWS)
        grads[b, m, :inner] = value.astype(jnp.bfloat16)
        if CORES * half > inner:
            grads[b, m, inner:] = jnp.zeros((CORES * half - inner, width), jnp.bfloat16)

    def pair_copy(b, m):
        other = pl.ds(pl.multiple_of((1 - core) * half, half), half)
        return pltpu.make_async_remote_copy(
            src_ref=grads.at[b, m, other], dst_ref=pair_in.at[b, m],
            send_sem=pair_send.at[b * 3 + m], recv_sem=pair_recv.at[b * 3 + m],
            device_id={"tok": mate}, device_id_type=MESH,
        )

    def line_copy(buf, b, m, owner, send, recv, to):
        return pltpu.make_async_remote_copy(
            src_ref=buf.at[b, m, in_half(owner)], dst_ref=buf.at[b, m, in_half(owner)],
            send_sem=send.at[b * 3 + m, owner], recv_sem=recv.at[b * 3 + m, owner],
            device_id={"tok": to}, device_id_type=MESH,
        )

    def right_copy(b, m, owner):
        return line_copy(from_left, b, m, owner, r_send, r_recv, right)

    def left_copy(b, m, owner):
        return line_copy(from_right, b, m, owner, l_send, l_recv, left)

    def share_copy(b, m, owner, of_core, send, recv, to):
        place = weights.at[b + 1, m, rows_of(owner, of_core)]
        return pltpu.make_async_remote_copy(
            src_ref=place, dst_ref=place,
            send_sem=send.at[b * 3 + m, owner], recv_sem=recv.at[b * 3 + m, owner],
            device_id={"tok": to}, device_id_type=MESH,
        )

    def own_term(b, m, owner):
        return (
            grads[b, m, rows_of(owner, core)].astype(jnp.float32)
            + pair_in[b, m, in_half(owner)].astype(jnp.float32)
        )

    def reduce_step(b, m, t):
        if t < line - 1:
            @pl.when(z <= t)
            def _():
                owner = line - 1 - t + z
                value = own_term(b, m, owner)

                @pl.when(z == 0)
                def _():
                    from_left[b, m, in_half(owner)] = value.astype(jnp.bfloat16)

                @pl.when(z > 0)
                def _():
                    right_copy(b, m, owner).wait_recv()
                    from_left[b, m, in_half(owner)] = (
                        value + from_left[b, m, in_half(owner)].astype(jnp.float32)
                    ).astype(jnp.bfloat16)

                right_copy(b, m, owner).start()

            @pl.when(line - 1 - z <= t)
            def _():
                owner = t - (line - 1) + z
                value = own_term(b, m, owner)

                @pl.when(z == line - 1)
                def _():
                    from_right[b, m, in_half(owner)] = value.astype(jnp.bfloat16)

                @pl.when(z < line - 1)
                def _():
                    left_copy(b, m, owner).wait_recv()
                    from_right[b, m, in_half(owner)] = (
                        value + from_right[b, m, in_half(owner)].astype(jnp.float32)
                    ).astype(jnp.bfloat16)

                left_copy(b, m, owner).start()

    def update(b, m):
        @pl.when(has_left)
        def _():
            right_copy(b, m, z).wait_recv()

        @pl.when(has_right)
        def _():
            left_copy(b, m, z).wait_recv()

        mine = in_half(z)

        @pl.when(jnp.logical_not(has_left))
        def _():
            from_left[b, m, mine] = jnp.zeros((share, width), jnp.bfloat16)

        @pl.when(jnp.logical_not(has_right))
        def _():
            from_right[b, m, mine] = jnp.zeros((share, width), jnp.bfloat16)

        total = (
            own_term(b, m, z)
            + from_left[b, m, mine].astype(jnp.float32)
            + from_right[b, m, mine].astype(jnp.float32)
        ) * grad_scale
        first = w_ref[m, rows_of(z, core)]
        if b == 0:
            moment, before = total, first
        else:
            moment, before = MOMENTUM_DECAY * mom_s[m] + total, cur_s[m]
        summed = before + moment
        after = summed * row_rms(first) / row_rms(summed)
        mom_s[m] = moment
        cur_s[m] = after
        weights[b + 1, m, rows_of(z, core)] = after.astype(jnp.bfloat16)

        @pl.when(has_right)
        def _():
            share_copy(b, m, z, core, agr_send, ag_recv, right).start()

        @pl.when(has_left)
        def _():
            share_copy(b, m, z, core, agl_send, ag_recv, left).start()

        share_copy(b, m, z, core, agp_send, agp_recv, mate).start()

    def gather_step(b, m, t):
        @pl.when(z >= t)
        def _():
            owner = z - t
            share_copy(b, m, owner, core, agr_send, ag_recv, right).wait_recv()

            @pl.when(has_right)
            def _():
                share_copy(b, m, owner, core, agr_send, ag_recv, right).start()

            share_copy(b, m, owner, core, agp_send, agp_recv, mate).start()

        @pl.when(z + t <= line - 1)
        def _():
            owner = z + t
            share_copy(b, m, owner, core, agl_send, ag_recv, left).wait_recv()

            @pl.when(has_left)
            def _():
                share_copy(b, m, owner, core, agl_send, ag_recv, left).start()

            share_copy(b, m, owner, core, agp_send, agp_recv, mate).start()

    def gather_end(b, m):
        for owner in range(line):
            share_copy(b, m, owner, 1 - core, agp_send, agp_recv, mate).wait_recv()

    def chunk_steps(b, m):
        def begin():
            pair_copy(b, m).wait_recv()
            reduce_step(b, m, 0)

        steps = [begin]
        steps += [functools.partial(reduce_step, b, m, t) for t in range(1, line - 1)]
        steps.append(functools.partial(update, b, m))
        steps += [functools.partial(gather_step, b, m, t) for t in range(1, line)]
        steps.append(functools.partial(gather_end, b, m))
        return steps

    def out_copy(b, to):
        return pltpu.make_async_remote_copy(
            src_ref=made.at[b, pl.ds(pl.multiple_of(to * slab, slab), slab)],
            dst_ref=out_ref.at[b, :, pl.ds(pl.multiple_of(head * width, width), width)],
            send_sem=out_send.at[b, to], recv_sem=out_recv.at[b, head],
            device_id={"head": to}, device_id_type=MESH,
        )

    def out_arrival(b, source):
        return pltpu.make_async_remote_copy(
            src_ref=made.at[b, pl.ds(0, slab)],
            dst_ref=out_ref.at[b, :, pl.ds(pl.multiple_of(source * width, width), width)],
            send_sem=out_send.at[b, source], recv_sem=out_recv.at[b, source],
            device_id={"head": source}, device_id_type=MESH,
        )

    def out_own(b):
        return pltpu.make_async_copy(
            made.at[b, pl.ds(pl.multiple_of(head * slab, slab), slab)],
            out_ref.at[b, :, pl.ds(pl.multiple_of(head * width, width), width)],
            out_send.at[b, head],
        )

    def out_part(b, step):
        to = lax.rem(head + step, head_count)
        rows = pl.ds(pl.multiple_of(to * slab, slab), slab)
        query = q_ref[b, rows]
        gate = dot(query, weights[b + 1, GATE, :inner], CONTRACT_LAST)
        up = dot(query, weights[b + 1, UP, :inner], CONTRACT_LAST)
        hidden = (jax.nn.silu(gate) * up).astype(jnp.bfloat16)
        made[b, rows] = dot(hidden, weights[b + 1, OUT, :inner], CONTRACT_LAST).astype(jnp.bfloat16)
        if step < head_count:
            out_copy(b, to).start()
        else:
            out_own(b).start()

    active = []

    def tick():
        for steps in list(active):
            steps.pop(0)()
            if not steps:
                active.remove(steps)

    def launch(b, m):
        grad_part(b, m)
        pair_copy(b, m).start()
        steps = chunk_steps(b, m)
        active.append(steps)
        return steps

    for name in ("k0", "w1", "w3"):
        loads[name].wait()
    round_weights(GATE)
    round_weights(UP)
    keys_part(0)
    loads["v0"].wait()
    scaled_part(0)
    loads["w2"].wait()
    round_weights(OUT)
    back_part(0)

    ends = jnp.where(has_left, 1, 0) + jnp.where(has_right, 1, 0)
    pl.semaphore_wait(barrier, head_count + ends)

    parts_left = []
    for b in range(blocks):
        if b == 0:
            plan = (GATE, UP, OUT)
            chunks = {}
            for place, m in enumerate(plan):
                if place:
                    for _ in range(SPACING):
                        tick()
                chunks[m] = launch(b, m)
        else:
            while chunks[GATE] or chunks[UP]:
                tick()
            loads[f"k{b}"].wait()
            loads[f"v{b}"].wait()
            keys_part(b)
            scaled_part(b)
            before, chunks = chunks, {}
            chunks[OUT] = launch(b, OUT)
            while before[OUT]:
                tick()
            back_part(b)
            chunks[GATE] = launch(b, GATE)
            loads[f"q{b - 1}"].wait()
            parts_left = [functools.partial(out_part, b - 1, step) for step in range(1, head_count + 1)]
            for _ in range(SPACING):
                tick()
                if parts_left:
                    parts_left.pop(0)()
            chunks[UP] = launch(b, UP)
            while parts_left:
                tick()
                parts_left.pop(0)()
    while active:
        tick()
    loads[f"q{blocks - 1}"].wait()
    for step in range(1, head_count + 1):
        out_part(blocks - 1, step)

    for b in range(blocks):
        for m in range(3):
            pair_copy(b, m).wait_send()
            for owner in range(line):
                @pl.when(jnp.logical_and(has_right, owner > z))
                def _():
                    right_copy(b, m, owner).wait_send()

                @pl.when(jnp.logical_and(has_left, owner < z))
                def _():
                    left_copy(b, m, owner).wait_send()

                @pl.when(jnp.logical_and(has_right, owner <= z))
                def _():
                    share_copy(b, m, owner, core, agr_send, ag_recv, right).wait_send()

                @pl.when(jnp.logical_and(has_left, owner >= z))
                def _():
                    share_copy(b, m, owner, core, agl_send, ag_recv, left).wait_send()

                share_copy(b, m, owner, core, agp_send, agp_recv, mate).wait_send()
        out_own(b).wait()
        for step in range(1, head_count):
            other = lax.rem(head + step, head_count)
            out_copy(b, other).wait_send()
            out_arrival(b, other).wait_recv()


def local(tok_count, head_count, queries, key_tokens, values, learn_rates, w_first, w_second, w_third):
    blocks, tokens, width = queries.shape
    inner = w_first.shape[1]
    line = tok_count // CORES
    share = -(-inner // (tok_count * 16)) * 16
    padded = share * tok_count
    half = share * line
    firsts = [w[0] for w in (w_first, w_second, w_third)]
    if padded > inner:
        firsts = [jnp.pad(w, ((0, padded - inner), (0, 0))) for w in firsts]
    bf16, f32 = jnp.bfloat16, jnp.float32
    dma = pltpu.SemaphoreType.DMA
    body = functools.partial(kernel, tok_count, head_count, share, inner)
    hbm = pl.BlockSpec(memory_space=pl.ANY)
    return pl.pallas_call(
        body,
        out_shape=jax.ShapeDtypeStruct((blocks, tokens // head_count, width * head_count), bf16),
        in_specs=[hbm, hbm, hbm, pl.BlockSpec(memory_space=pltpu.VMEM), hbm, hbm, hbm],
        out_specs=hbm,
        scratch_shapes=[
            pltpu.VMEM((blocks, tokens, width), bf16),
            pltpu.VMEM((blocks, tokens, width), bf16),
            pltpu.VMEM((blocks, tokens, width), bf16),
            pltpu.VMEM((3, padded, width), f32),
            pltpu.VMEM((blocks + 1, 3, padded, width), bf16),
            pltpu.VMEM((tokens, inner), f32),
            pltpu.VMEM((tokens, inner), f32),
            pltpu.VMEM((tokens, width), bf16),
            pltpu.VMEM((tokens, inner), bf16),
            pltpu.VMEM((tokens, inner), bf16),
            pltpu.VMEM((tokens, inner), bf16),
            pltpu.VMEM((blocks, 3, padded, width), bf16),
            pltpu.VMEM((blocks, 3, half, width), bf16),
            pltpu.VMEM((blocks, 3, half, width), bf16),
            pltpu.VMEM((blocks, 3, half, width), bf16),
            pltpu.VMEM((3, share, width), f32),
            pltpu.VMEM((3, share, width), f32),
            pltpu.VMEM((blocks, tokens, width), bf16),
            dma((3 + 3 * blocks,)),
            dma((3 * blocks,)),
            dma((3 * blocks,)),
        ]
        + [dma((3 * blocks, line)) for _ in range(9)]
        + [dma((blocks, head_count)) for _ in range(2)],
        compiler_params=pltpu.CompilerParams(
            collective_id=0, has_side_effects=True, vmem_limit_bytes=56 * 1024 * 1024
        ),
    )(queries, key_tokens, values, learn_rates, *firsts)


def solution(mesh):
    placed = (
        P(None, ("grp", "tok"), "head"),
        P(None, ("grp", "tok"), "head"),
        P(None, ("grp", "tok"), "head"),
        P(None, "head", ("grp", "tok")),
        P("head", None, None),
        P("head", None, None),
        P("head", None, None),
    )
    return jax.shard_map(
        functools.partial(local, mesh.shape["tok"], mesh.shape["head"]),
        mesh=mesh,
        in_specs=placed,
        out_specs=P(None, ("grp", "tok", "head"), None),
        check_vma=False,
    )
```

```python
import functools
import math

import jax
import jax.numpy as jnp
from jax import lax
from jax.experimental import pallas as pl
from jax.experimental.pallas import tpu as pltpu
from jax.sharding import PartitionSpec as P

MOMENTUM_DECAY = 0.9
EPSILON = 1e-06
CONTRACT_ROWS = (((0,), (0,)), ((), ()))
CONTRACT_LAST = (((1,), (1,)), ((), ()))
MESH = pl.DeviceIdType.MESH
CORES = 2
GATE, OUT, UP = 0, 1, 2
CHUNKS = 4
LAG = 3


def row_rms(matrix):
    return jnp.sqrt(jnp.mean(matrix * matrix, axis=-1, keepdims=True) + EPSILON)


def dot(lhs, rhs, dims):
    return lax.dot_general(lhs, rhs, dims, preferred_element_type=jnp.float32)


def kernel(
    tok_count, head_count, chunks, pieces, inner,
    q_hbm, k_hbm, v_hbm, rates_ref, w1_hbm, w2_hbm, w3_hbm, out_ref,
    q_ref, k_ref, v_ref, w_ref, weights, silu_s, slope_s, e_s, z_s, ga_s, gb_s,
    grads, pair_in, partial, from_outer, from_cross, cur_s, mom_s, made,
    load_sem, pair_send, pair_recv, in_send, outer_recv, cross_recv,
    w_send, w_recv, m_send, m_recv, out_send, out_recv,
):
    line = tok_count // CORES
    half = inner // CORES
    chunk = half // chunks
    deepest = line // 2 - 1
    blocks, tokens, width = q_ref.shape
    slab = tokens // head_count
    piece = slab // pieces
    tile = min(256, tokens)
    grad_scale = 1.0 / math.sqrt(tokens * tok_count)
    tok = lax.axis_index("tok")
    head = lax.axis_index("head")
    z = tok // CORES
    core = lax.rem(tok, CORES)
    mate = tok + 1 - 2 * core
    is_low = z <= deepest
    depth = jnp.where(is_low, z, line - 1 - z)
    inward = jnp.where(is_low, tok + CORES, tok - CORES)
    outward = jnp.where(is_low, tok - CORES, tok + CORES)

    def rows_of(of_core, c):
        return pl.ds(pl.multiple_of(of_core * half + c * chunk, 16), chunk)

    def in_half(c):
        return pl.ds(c * chunk, chunk)

    barrier = pltpu.get_barrier_semaphore()

    @pl.when(depth > 0)
    def _():
        pl.semaphore_signal(barrier, inc=1, device_id={"tok": outward}, device_id_type=MESH)

    pl.semaphore_signal(barrier, inc=1, device_id={"tok": inward}, device_id_type=MESH)
    pl.semaphore_signal(barrier, inc=1, device_id={"tok": mate}, device_id_type=MESH)
    for step in range(1, head_count):
        pl.semaphore_signal(
            barrier, inc=1, device_id={"head": lax.rem(head + step, head_count)}, device_id_type=MESH
        )

    loads = {}
    order = [
        ("k0", k_hbm.at[0], k_ref.at[0]),
        ("w1", w1_hbm, w_ref.at[GATE]),
        ("w3", w3_hbm, w_ref.at[UP]),
        ("v0", v_hbm.at[0], v_ref.at[0]),
        ("w2", w2_hbm, w_ref.at[OUT]),
    ]
    for b in range(1, blocks):
        order.append((f"k{b}", k_hbm.at[b], k_ref.at[b]))
        order.append((f"v{b}", v_hbm.at[b], v_ref.at[b]))
    for b in range(blocks):
        order.append((f"q{b}", q_hbm.at[b], q_ref.at[b]))
    for place, (name, src, dst) in enumerate(order):
        loads[name] = pltpu.make_async_copy(src, dst, load_sem.at[place])
        loads[name].start()

    def round_weights(m):
        weights[0, m] = w_ref[m].astype(jnp.bfloat16)

    def keys_part(b):
        @pl.loop(0, tokens // tile)
        def _(i):
            rows = pl.ds(pl.multiple_of(i * tile, tile), tile)
            keys = k_ref[b, rows]
            gate = dot(keys, weights[b, GATE], CONTRACT_LAST)
            up = dot(keys, weights[b, UP], CONTRACT_LAST)
            sig = jax.nn.sigmoid(gate)
            silu = gate * sig
            z_s[rows] = (silu * up).astype(jnp.bfloat16)
            silu_s[rows] = silu
            slope_s[rows] = up * (sig * (1.0 + gate * (1.0 - sig)))

    def scaled_part(b):
        lanes = math.gcd(width, 128)
        for i in range(tokens // tile):
            rows = pl.ds(i * tile, tile)
            rate = jnp.transpose(jnp.broadcast_to(rates_ref[b, :, rows], (lanes, tile)))
            for j in range(width // lanes):
                cols = pl.ds(j * lanes, lanes)
                e_s[rows, cols] = (rate * v_ref[b, rows, cols].astype(jnp.float32)).astype(jnp.bfloat16)

    def back_part(b):
        @pl.loop(0, tokens // tile)
        def _(i):
            rows = pl.ds(pl.multiple_of(i * tile, tile), tile)
            back = lax.dot_general(
                e_s[rows], weights[b, OUT], (((1,), (0,)), ((), ())),
                preferred_element_type=jnp.float32,
            )
            ga_s[rows] = (back * slope_s[rows]).astype(jnp.bfloat16)
            gb_s[rows] = (back * silu_s[rows]).astype(jnp.bfloat16)

    def grad_part(b, m):
        if m == GATE:
            value = dot(ga_s[...], k_ref[b], CONTRACT_ROWS)
        elif m == OUT:
            value = dot(e_s[...], z_s[...], CONTRACT_ROWS)
        else:
            value = dot(gb_s[...], k_ref[b], CONTRACT_ROWS)
        grads[b, m] = value.astype(jnp.bfloat16)

    def pair_copy(b, m, c):
        return pltpu.make_async_remote_copy(
            src_ref=grads.at[b, m, rows_of(1 - core, c)], dst_ref=pair_in.at[b, m, in_half(c)],
            send_sem=pair_send.at[b * 3 + m, c], recv_sem=pair_recv.at[b * 3 + m, c],
            device_id={"tok": mate}, device_id_type=MESH,
        )

    def sum_copy(b, m, c, into, recv):
        return pltpu.make_async_remote_copy(
            src_ref=partial.at[b, m, in_half(c)], dst_ref=into.at[b, m, in_half(c)],
            send_sem=in_send.at[b * 3 + m, c], recv_sem=recv.at[b * 3 + m, c],
            device_id={"tok": inward}, device_id_type=MESH,
        )

    def inward_copy(b, m, c):
        return sum_copy(b, m, c, from_outer, outer_recv)

    def cross_copy(b, m, c):
        return sum_copy(b, m, c, from_cross, cross_recv)

    def weight_copy(b, m, c, of_core, send, recv, to):
        place = weights.at[b + 1, m, rows_of(of_core, c)]
        return pltpu.make_async_remote_copy(
            src_ref=place, dst_ref=place,
            send_sem=send.at[b * 3 + m, c], recv_sem=recv.at[b * 3 + m, c],
            device_id={"tok": to}, device_id_type=MESH,
        )

    def outward_copy(b, m, c):
        return weight_copy(b, m, c, core, w_send, w_recv, outward)

    def mate_copy(b, m, c, of_core):
        return weight_copy(b, m, c, of_core, m_send, m_recv, mate)

    def sum_step(b, m, c, t):
        if t == 0:
            pair_copy(b, m, c).wait_recv()

        @pl.when(depth == t)
        def _():
            value = (
                grads[b, m, rows_of(core, c)].astype(jnp.float32)
                + pair_in[b, m, in_half(c)].astype(jnp.float32)
            )
            if t > 0:
                inward_copy(b, m, c).wait_recv()
                value = value + from_outer[b, m, in_half(c)].astype(jnp.float32)
            partial[b, m, in_half(c)] = value.astype(jnp.bfloat16)
            if t == deepest:
                cross_copy(b, m, c).start()
            else:
                inward_copy(b, m, c).start()

    def send_weights(b, m, c):
        @pl.when(depth > 0)
        def _():
            outward_copy(b, m, c).start()

        mate_copy(b, m, c, core).start()

    def update(b, m, c):
        @pl.when(depth == deepest)
        def _():
            cross_copy(b, m, c).wait_recv()
            total = (
                partial[b, m, in_half(c)].astype(jnp.float32)
                + from_cross[b, m, in_half(c)].astype(jnp.float32)
            ) * grad_scale
            first = w_ref[m, rows_of(core, c)]
            if b == 0:
                moment, before = total, first
            else:
                moment = MOMENTUM_DECAY * mom_s[m, in_half(c)] + total
                before = cur_s[m, in_half(c)]
            summed = before + moment
            after = summed * row_rms(first) / row_rms(summed)
            mom_s[m, in_half(c)] = moment
            cur_s[m, in_half(c)] = after
            weights[b + 1, m, rows_of(core, c)] = after.astype(jnp.bfloat16)
            send_weights(b, m, c)

    def weight_step(b, m, c, t):
        @pl.when(depth == deepest - t)
        def _():
            outward_copy(b, m, c).wait_recv()
            send_weights(b, m, c)

    def weight_end(b, m, c):
        mate_copy(b, m, c, 1 - core).wait_recv()

    def chunk_steps(b, m, c):
        steps = [functools.partial(sum_step, b, m, c, t) for t in range(deepest + 1)]
        steps.append(functools.partial(update, b, m, c))
        steps += [functools.partial(weight_step, b, m, c, t) for t in range(1, deepest + 1)]
        steps.append(functools.partial(weight_end, b, m, c))
        return steps

    def out_rows(to, p):
        return pl.ds(pl.multiple_of(to * slab + p * piece, 16), piece)

    def out_place(b, source, p):
        columns = pl.ds(pl.multiple_of(source * width, width), width)
        return out_ref.at[b, pl.ds(p * piece, piece), columns]

    def out_copy(b, to, p):
        return pltpu.make_async_remote_copy(
            src_ref=made.at[b, out_rows(to, p)], dst_ref=out_place(b, head, p),
            send_sem=out_send.at[b * pieces + p, to], recv_sem=out_recv.at[b * pieces + p, head],
            device_id={"head": to}, device_id_type=MESH,
        )

    def out_arrival(b, source, p):
        return pltpu.make_async_remote_copy(
            src_ref=made.at[b, out_rows(source, p)], dst_ref=out_place(b, source, p),
            send_sem=out_send.at[b * pieces + p, source], recv_sem=out_recv.at[b * pieces + p, source],
            device_id={"head": source}, device_id_type=MESH,
        )

    def out_own(b, p):
        return pltpu.make_async_copy(
            made.at[b, out_rows(head, p)], out_place(b, head, p), out_send.at[b * pieces + p, head]
        )

    def query_part(b, i):
        rows = pl.ds(i * tile, tile)
        silu_s[rows] = jax.nn.silu(dot(q_ref[b, rows], weights[b + 1, GATE], CONTRACT_LAST))

    def out_part(b, step, p):
        to = lax.rem(head + step, head_count)
        rows = out_rows(to, p)
        up = dot(q_ref[b, rows], weights[b + 1, UP], CONTRACT_LAST)
        hidden = (silu_s[rows] * up).astype(jnp.bfloat16)
        made[b, rows] = dot(hidden, weights[b + 1, OUT], CONTRACT_LAST).astype(jnp.bfloat16)
        if step < head_count:
            out_copy(b, to, p).start()
        else:
            out_own(b, p).start()

    def out_parts(b):
        return [
            functools.partial(out_part, b, step, p)
            for step in range(1, head_count + 1)
            for p in range(pieces)
        ]

    waiting, active, ended = [], [], set()

    def tick():
        for entry in list(active):
            if entry[1] % LAG == 0:
                entry[2].pop(0)()
            entry[1] += 1
            if not entry[2]:
                active.remove(entry)
                ended.add(entry[0])
        if waiting:
            name = waiting.pop(0)
            steps = chunk_steps(*name)
            steps.pop(0)()
            active.append([name, 1, steps])

    def ticks(count):
        for _ in range(count):
            tick()

    def launch(b, m):
        grad_part(b, m)
        for c in range(chunks):
            pair_copy(b, m, c).start()
            waiting.append((b, m, c))

    def finish(b, *which):
        while any((b, m, c) not in ended for m in which for c in range(chunks)):
            tick()

    for name in ("k0", "w1", "w3"):
        loads[name].wait()
    round_weights(GATE)
    round_weights(UP)
    keys_part(0)
    loads["v0"].wait()
    scaled_part(0)
    loads["w2"].wait()
    round_weights(OUT)
    back_part(0)
    pl.semaphore_wait(barrier, head_count + 1 + jnp.where(depth > 0, 1, 0))
    launch(0, GATE)
    launch(0, UP)
    ticks(2)
    launch(0, OUT)
    for name in [name for name in loads if name[0] in "kvq" and name not in ("k0", "v0")]:
        loads[name].wait()
    for b in range(1, blocks):
        ticks(chunks)
        scaled_part(b)
        finish(b - 1, GATE, UP)
        keys_part(b)
        launch(b, OUT)
        finish(b - 1, OUT)
        ticks(1)
        back_part(b)
        launch(b, GATE)
        launch(b, UP)
        ticks(2)
        for i in range(tokens // tile):
            query_part(b - 1, i)
            tick()
        for part in out_parts(b - 1):
            part()
            tick()
    finish(blocks - 1, OUT, GATE)
    for i in range(tokens // tile):
        query_part(blocks - 1, i)
        tick()
    finish(blocks - 1, UP)
    for part in out_parts(blocks - 1):
        part()

    for b in range(blocks):
        for m in range(3):
            for c in range(chunks):
                pair_copy(b, m, c).wait_send()
                cross_copy(b, m, c).wait_send()
                mate_copy(b, m, c, core).wait_send()

                @pl.when(depth > 0)
                def _():
                    outward_copy(b, m, c).wait_send()

        for p in range(pieces):
            out_own(b, p).wait()
            for step in range(1, head_count):
                other = lax.rem(head + step, head_count)
                out_copy(b, other, p).wait_send()
                out_arrival(b, other, p).wait_recv()


def local(tok_count, head_count, queries, key_tokens, values, learn_rates, w_first, w_second, w_third):
    blocks, tokens, width = queries.shape
    inner = w_first.shape[1]
    half = inner // CORES
    chunks = next(n for n in (CHUNKS, 2, 1) if half % (n * 16) == 0)
    slab = tokens // head_count
    pieces = 2 if slab % 256 == 0 else 1
    firsts = [w[0] for w in (w_first, w_second, w_third)]
    bf16, f32 = jnp.bfloat16, jnp.float32
    dma = pltpu.SemaphoreType.DMA
    body = functools.partial(kernel, tok_count, head_count, chunks, pieces, inner)
    hbm = pl.BlockSpec(memory_space=pl.ANY)
    return pl.pallas_call(
        body,
        out_shape=jax.ShapeDtypeStruct((blocks, tokens // head_count, width * head_count), bf16),
        in_specs=[hbm, hbm, hbm, pl.BlockSpec(memory_space=pltpu.VMEM), hbm, hbm, hbm],
        out_specs=hbm,
        scratch_shapes=[
            pltpu.VMEM((blocks, tokens, width), bf16),
            pltpu.VMEM((blocks, tokens, width), bf16),
            pltpu.VMEM((blocks, tokens, width), bf16),
            pltpu.VMEM((3, inner, width), f32),
            pltpu.VMEM((blocks + 1, 3, inner, width), bf16),
            pltpu.VMEM((tokens, inner), f32),
            pltpu.VMEM((tokens, inner), f32),
            pltpu.VMEM((tokens, width), bf16),
            pltpu.VMEM((tokens, inner), bf16),
            pltpu.VMEM((tokens, inner), bf16),
            pltpu.VMEM((tokens, inner), bf16),
            pltpu.VMEM((blocks, 3, inner, width), bf16),
            pltpu.VMEM((blocks, 3, half, width), bf16),
            pltpu.VMEM((blocks, 3, half, width), bf16),
            pltpu.VMEM((blocks, 3, half, width), bf16),
            pltpu.VMEM((blocks, 3, half, width), bf16),
            pltpu.VMEM((3, half, width), f32),
            pltpu.VMEM((3, half, width), f32),
            pltpu.VMEM((blocks, tokens, width), bf16),
            dma((3 + 3 * blocks,)),
        ]
        + [dma((3 * blocks, chunks)) for _ in range(9)]
        + [dma((blocks * pieces, head_count)) for _ in range(2)],
        compiler_params=pltpu.CompilerParams(
            collective_id=0, has_side_effects=True, vmem_limit_bytes=56 * 1024 * 1024
        ),
    )(queries, key_tokens, values, learn_rates, *firsts)


def solution(mesh):
    placed = (
        P(None, ("grp", "tok"), "head"),
        P(None, ("grp", "tok"), "head"),
        P(None, ("grp", "tok"), "head"),
        P(None, "head", ("grp", "tok")),
        P("head", None, None),
        P("head", None, None),
        P("head", None, None),
    )
    return jax.shard_map(
        functools.partial(local, mesh.shape["tok"], mesh.shape["head"]),
        mesh=mesh,
        in_specs=placed,
        out_specs=P(None, ("grp", "tok", "head"), None),
        check_vma=False,
    )
```
